32 devices in a mesh: parts: 2 (over x), blk: 16 (over z, y, core).
Axes of the slice: x: 2, y: 2, z: 4, core: 2. Of those that a mesh axis runs over, the one named last changes fastest.
Arguments:
- queries: bfloat16 [256, 4096], P(('parts', 'blk')), parts along dimension 0, may hold values from -48 to 48
- key_cache: bfloat16 [8192, 512], P(('parts', 'blk')), parts along dimension 0, may hold values from -6 to 6
- value_cache: bfloat16 [8192, 512], P(('parts', 'blk')), parts along dimension 0, may hold values from -6 to 6
- tile_page: int32 [8192], P(('parts', 'blk')), parts along dimension 0, may hold values from 0 to 15, never falling along the last dimension, each value on 1 to 512 neighbouring positions
- row_last: int32 [256], P(('parts', 'blk')), parts along dimension 0, may hold values from 0 to 15, as said below
Outputs:
- attention_out: bfloat16 [256, 4096], P(('parts', 'blk')), parts along dimension 0
The draws below stay inside these ranges and needn't reach their ends.
There are 2 independent parts, one for each index of `parts`. The reference program is written for one: setup_inputs(seed, part) draws one part's arguments, and reference() takes and returns one part's arrays. A program takes and returns all parts, laid end to end along the dimension named above; each array names one. Nothing has to cross between parts.
Inputs may be any that keep to these rules, and one draw needn't show every extreme that they name: tile_page never falls along the tile tokens; every page of 0 to 15 has between 1 and 512 tokens, one exactly 512. row_last never falls along the text rows; the first row sees page 0 only and the last row sees every page.
All inputs are finite; a program needn't handle non-finite values.
Results may differ from the reference program's by a relative error of at most 0.00575.
Values may be sent and summed in bfloat16 or wider, within the bound.
A program may use at most 64 MiB of HBM per device.

```python
import math
import jax
import jax.numpy as jnp
import numpy as np
from jax import lax

HEADS = 32
KV_HEADS = 4
HEAD_DIM = 128
TILE_DEV = 256
ROWS_DEV = 8
PAGES = 16
TILES = 4096
TEXT = 128
N_BLK = 16


def joint_draw(key):
    base_key = jax.random.fold_in(key, 7001)
    query_key, cache_key = jax.random.split(base_key, 2)
    group_size = HEADS // KV_HEADS
    cache_heads = jnp.clip(jax.random.normal(cache_key, (TILES, KV_HEADS, HEAD_DIM), jnp.float32), -6.0, 6.0)
    query_heads = jnp.clip(jax.random.normal(query_key, (TEXT, KV_HEADS, group_size, HEAD_DIM), jnp.float32), -6.0, 6.0)
    query_flat = query_heads.reshape(TEXT, HEADS * HEAD_DIM).astype(jnp.bfloat16)
    cache_flat = cache_heads.reshape(TILES, KV_HEADS * HEAD_DIM).astype(jnp.bfloat16)
    return (query_flat, cache_flat)


def draw_queries(key, part):
    return joint_draw(key)[0]


def draw_key_cache(key, part):
    return joint_draw(key)[1]


def draw_row_last(key, part):
    drawn = jax.random.randint(jax.random.fold_in(key, 9103), (TEXT,), 0, PAGES)
    ordered = jnp.sort(drawn)
    ordered = ordered.at[0].set(0).at[TEXT - 1].set(PAGES - 1)
    return ordered.astype(jnp.int32)


def levels(own_key, dims, shards, smallest, largest):
    gain, own = 1.0, jax.random.fold_in(own_key, 6)
    for dim, blocks in shards:
        draws = jnp.exp(jax.random.uniform(jax.random.fold_in(own, dim), (blocks,), jnp.float32, smallest / len(shards), largest / len(shards)))
        gain = gain * jnp.repeat(draws, dims[dim] // blocks).reshape([-1 if axis == dim else 1 for axis in range(len(dims))])
    return gain


def split_up(number_of, total, most, slope):
    weights = [(1 << 20) // math.isqrt(rank ** slope) + 1 for rank in range(2, number_of + 1)]
    spare, holding = total - most - (number_of - 1), [1] * (number_of - 1)
    while spare > 0:
        candidates = [i for i in range(number_of - 1) if holding[i] < most]
        whole, budget = sum([weights[i] for i in candidates]), spare
        for i in candidates:
            more = min(most - holding[i], max(1, budget * weights[i] // whole), spare)
            holding[i] = holding[i] + more
            spare = spare - more
    return np.array([most] + holding)


def ragged(own_key, count, total, limit, slope):
    if count == 2:
        one = jax.random.randint(own_key, (), max(1, total - limit), min(limit, total - 1) + 1)
        return jnp.stack([one, total - one])
    lengths = jnp.asarray(split_up(count, total, limit, slope), jnp.int32)
    twos = (count - 1) // 2
    donor, taker = lengths[1:1 + 2 * twos:2], lengths[2:2 + 2 * twos:2]
    slack = jnp.minimum(donor - 1, limit - taker)
    shifted = jax.random.randint(jax.random.fold_in(own_key, 1), (twos,), 0, 1 << 20) % (slack + 1)
    lengths = lengths.at[1:1 + 2 * twos:2].set(donor - shifted).at[2:2 + 2 * twos:2].set(taker + shifted)
    return lengths[jax.random.permutation(jax.random.fold_in(own_key, 2), count)]


def centred(stream_key, shape, spread, reach, pieces=(), dtype=jnp.bfloat16):
    values = jax.random.normal(stream_key, shape, jnp.float32) * spread
    if len(pieces) > 0:
        values = levels(stream_key, shape, pieces, -0.22, 0.18) * values
    return jnp.clip(values, min=-reach, max=reach).astype(dtype)


def setup_inputs(seed: int = 0, part: int = 0) -> dict:
    key_of = jax.random.split(jax.random.key(seed), 6)
    part_keys = jax.random.split(jax.random.fold_in(key_of[5], part), 6)
    return {
        "queries": draw_queries(jax.random.fold_in(jax.random.fold_in(key_of[5], part), 71), part),
        "key_cache": draw_key_cache(jax.random.fold_in(jax.random.fold_in(key_of[5], part), 71), part),
        "value_cache": centred(part_keys[2], (TILES, KV_HEADS * HEAD_DIM), 1.0, 6.0, ((0, 16),)),
        "tile_page": jnp.searchsorted(jnp.cumsum(ragged(part_keys[3], PAGES, TILES, 2 * TILE_DEV, 1)), jnp.arange(TILES), side="right").astype(jnp.int32),
        "row_last": draw_row_last(jax.random.fold_in(jax.random.fold_in(key_of[5], part), 71), part),
    }


NEGATIVE_FILL = -1e+30

def reference(queries, key_cache, value_cache, tile_page, row_last):
    group_size = HEADS // KV_HEADS
    score_scale = 1.0 / math.sqrt(HEAD_DIM)
    key_heads = key_cache.reshape(TILES, KV_HEADS, HEAD_DIM).astype(jnp.float32)
    value_heads = value_cache.reshape(TILES, KV_HEADS, HEAD_DIM).astype(jnp.float32)
    query_blocks = queries.reshape(N_BLK, ROWS_DEV, KV_HEADS, group_size, HEAD_DIM)
    last_blocks = row_last.reshape(N_BLK, ROWS_DEV)

    def attend_block(block_pair):
        query_rows, last_rows = block_pair
        scores = jnp.einsum('rkgd,tkd->rkgt', query_rows.astype(jnp.float32), key_heads) * score_scale
        visible = (tile_page[None, :] <= last_rows[:, None])[:, None, None, :]
        masked = jnp.where(visible, scores, NEGATIVE_FILL)
        row_top = lax.optimization_barrier(jnp.max(masked, axis=-1, keepdims=True))
        weights = jnp.where(visible, jnp.exp(scores - row_top), 0.0)
        weight_total = lax.optimization_barrier(jnp.sum(weights, axis=-1))
        rounded = lax.optimization_barrier(weights.astype(jnp.bfloat16))
        attended = jnp.einsum('rkgt,tkd->rkgd', rounded.astype(jnp.float32), value_heads)
        result = (attended / weight_total[..., None]).astype(jnp.bfloat16)
        return result.reshape(ROWS_DEV, HEADS * HEAD_DIM)
    blocks_out = lax.map(attend_block, (query_blocks, last_blocks))
    return blocks_out.reshape(TEXT, HEADS * HEAD_DIM)
```

```python
import functools
import math

import jax
import jax.numpy as jnp
from jax import lax
from jax.experimental import pallas as pl
from jax.experimental.pallas import tpu as pltpu
from jax.sharding import PartitionSpec as P

KV_HEADS = 4
HEAD_DIM = 128
NEGATIVE_FILL = -1e30
LOG2E = math.log2(math.e)
MESH = pl.DeviceIdType.MESH


def each(count, body):
    if count <= 4:
        for i in range(count):
            body(i)
    else:
        lax.fori_loop(0, count, lambda i, c: (body(i), c)[1], 0)


def kernel(
    groups, q_hbm, k_hbm, v_hbm, page_ref, last_ref, out_ref,
    q_in, k_in, v_in, q_pack, v_turned, meta_mine,
    q_all, k_all, v_all, meta_all, last_all, page_col,
    part_mine, part_all, lse_mine, lse_all, res, fin,
    in_sem, q_send, q_recv, m_send, m_recv, k_send, k_recv, v_send, v_recv,
    qz_send, qz_recv, mz_send, mz_recv, o_send, o_recv, l_send, l_recv, f_send, f_recv,
):
    part, me = lax.axis_index("parts"), lax.axis_index("blk")
    member, group = lax.rem(me, KV_HEADS), lax.div(me, KV_HEADS)
    rows = q_in.shape[0]
    heads = q_in.shape[1] // HEAD_DIM
    tokens = k_in.shape[0]
    per_group = heads // KV_HEADS
    block = per_group * rows

    mates = [lax.rem(member + d, KV_HEADS) for d in (2, 1, 3)]
    mate_ids = [group * KV_HEADS + m for m in mates]
    order = sorted(range(1, groups), key=lambda s: -min(s, groups - s))

    def peer(i):
        if groups <= 4:
            return lax.rem(group + order[i], groups)
        return lax.rem(group + 1 + i, groups)

    def copy(src, dst, send, recv, target):
        return pltpu.make_async_remote_copy(
            src_ref=src, dst_ref=dst, send_sem=send, recv_sem=recv,
            device_id=(part, target), device_id_type=MESH,
        )

    load_q = pltpu.make_async_copy(q_hbm, q_in, in_sem.at[0])
    load_k = pltpu.make_async_copy(k_hbm, k_in, in_sem.at[1])
    load_v = pltpu.make_async_copy(v_hbm, v_in, in_sem.at[2])
    load_q.start()
    load_k.start()
    load_v.start()

    barrier = pltpu.get_barrier_semaphore()
    for target in mate_ids:
        pl.semaphore_signal(barrier, inc=1, device_id=(part, target), device_id_type=MESH)

    def greet(i):
        target = peer(i) * KV_HEADS + member
        pl.semaphore_signal(barrier, inc=1, device_id=(part, target), device_id_type=MESH)

    each(groups - 1, greet)

    lane = lax.broadcasted_iota(jnp.int32, (1, 128), 1)
    pattern = jnp.zeros((1, 128), jnp.int32)
    for r in range(rows):
        pattern = jnp.where(lax.rem(lane, rows) == r, last_ref[r], pattern)
    meta_mine[:, :128] = pattern
    meta_mine[:, 128:] = page_ref[...]
    meta_all[member] = meta_mine[...]

    load_q.wait()
    wide = q_in[...].astype(jnp.float32)
    stacked = jnp.concatenate(
        [wide[:, h * HEAD_DIM:(h + 1) * HEAD_DIM] for h in range(heads)], axis=0
    )
    q_pack[...] = stacked.astype(jnp.bfloat16).reshape(KV_HEADS, block, HEAD_DIM)
    q_all[group, member] = q_pack[member]
    load_k.wait()

    pl.semaphore_wait(barrier, KV_HEADS - 1 + groups - 1)

    q_copies, m_copies, k_copies = [], [], []
    for i, (m, target) in enumerate(zip(mates, mate_ids)):
        q_copies.append(copy(q_pack.at[m], q_all.at[group, member], q_send.at[i], q_recv.at[member], target))
        q_copies[-1].start()
        m_copies.append(copy(meta_mine, meta_all.at[member], m_send.at[i], m_recv.at[member], target))
        m_copies[-1].start()
    for i, (m, target) in enumerate(zip(mates, mate_ids)):
        columns = pl.ds(pl.multiple_of(m * HEAD_DIM, HEAD_DIM), HEAD_DIM)
        k_copies.append(copy(k_in.at[:, columns], k_all.at[member], k_send.at[i], k_recv.at[member], target))
        k_copies[-1].start()

    load_v.wait()
    v_turned[...] = (
        v_in[...].astype(jnp.float32).T.astype(jnp.bfloat16).reshape(KV_HEADS, HEAD_DIM, tokens)
    )
    v_copies = []
    for i, (m, target) in enumerate(zip(mates, mate_ids)):
        v_copies.append(copy(v_turned.at[m], v_all.at[member], v_send.at[i], v_recv.at[member], target))
        v_copies[-1].start()

    for m, target in zip(mates, mate_ids):
        copy(q_all.at[group, m], q_all.at[group, m], q_send.at[0], q_recv.at[m], target).wait_recv()
        copy(meta_all.at[m], meta_all.at[m], m_send.at[0], m_recv.at[m], target).wait_recv()
    last_all[group] = meta_all[:, :, :128]

    def q_copy(i):
        target = peer(i) * KV_HEADS + member
        return copy(q_all.at[group], q_all.at[group], qz_send.at[i], qz_recv.at[group], target)

    def m_copy(i):
        target = peer(i) * KV_HEADS + member
        return copy(last_all.at[group], last_all.at[group], mz_send.at[i], mz_recv.at[group], target)

    def forward(i):
        m_copy(i).start()
        q_copy(i).start()

    each(groups - 1, forward)

    own = pl.ds(pl.multiple_of(member * HEAD_DIM, HEAD_DIM), HEAD_DIM)
    k_all[member] = k_in[:, own]
    v_all[member] = v_turned[member]
    for s in range(KV_HEADS):
        pages = meta_all[s][:, 128:].astype(jnp.float32)
        page_col[s] = jnp.broadcast_to(pages, (HEAD_DIM, tokens)).T

    for m, target in zip(mates, mate_ids):
        copy(k_all.at[m], k_all.at[m], k_send.at[0], k_recv.at[m], target).wait_recv()
    for m, target in zip(mates, mate_ids):
        copy(v_all.at[m], v_all.at[m], v_send.at[0], v_recv.at[m], target).wait_recv()

    factor = LOG2E / math.sqrt(HEAD_DIM)

    def attend(which):
        lasts = last_all[which].astype(jnp.float32)
        per_row = 128 // block
        pieces = []
        for first in range(0, KV_HEADS, per_row):
            piece = lasts[first]
            for k in range(1, per_row):
                piece = jnp.where(lane < k * block, piece, lasts[first + k])
            pieces.append(piece)
        last_row = jnp.concatenate(pieces, axis=1)
        queries = q_all[which].reshape(KV_HEADS * block, HEAD_DIM)
        masked = []
        for s in range(KV_HEADS):
            scores = lax.dot_general(
                k_all[s], queries, (((1,), (1,)), ((), ())), preferred_element_type=jnp.float32
            )
            column = page_col[s]
            pages = jnp.concatenate([column] * len(pieces), axis=1)
            masked.append(jnp.where(pages <= last_row, scores, NEGATIVE_FILL))
        top = functools.reduce(jnp.maximum, [jnp.max(x, axis=0, keepdims=True) for x in masked])
        total = jnp.zeros_like(top)
        out = jnp.zeros((HEAD_DIM, KV_HEADS * block), jnp.float32)
        for s in range(KV_HEADS):
            weights = jnp.exp2((masked[s] - top) * factor)
            total = total + jnp.sum(weights, axis=0, keepdims=True)
            out = out + jnp.dot(
                v_all[s], weights.astype(jnp.bfloat16), preferred_element_type=jnp.float32
            )
        return (out / total).astype(jnp.bfloat16), top * factor + jnp.log(total) * LOG2E

    def o_copy(i):
        to = peer(i)
        target = to * KV_HEADS + member
        return copy(part_mine.at[to], part_all.at[group], o_send.at[i], o_recv.at[group], target)

    def l_copy(i):
        to = peer(i)
        target = to * KV_HEADS + member
        return copy(lse_mine.at[to], lse_all.at[group], l_send.at[i], l_recv.at[group], target)

    def work(i):
        other = peer(i)
        target = other * KV_HEADS + member
        copy(last_all.at[other], last_all.at[other], mz_send.at[0], mz_recv.at[other], target).wait_recv()
        copy(q_all.at[other], q_all.at[other], qz_send.at[0], qz_recv.at[other], target).wait_recv()
        out, lse = attend(other)
        part_mine[other] = out
        lse_mine[other] = lse
        l_copy(i).start()
        o_copy(i).start()

    each(groups - 1, work)
    out, lse = attend(group)
    part_all[group] = out
    lse_all[group] = lse

    def arrive(i):
        other = peer(i)
        target = other * KV_HEADS + member
        copy(lse_all.at[other], lse_all.at[other], l_send.at[0], l_recv.at[other], target).wait_recv()
        copy(part_all.at[other], part_all.at[other], o_send.at[0], o_recv.at[other], target).wait_recv()

    each(groups - 1, arrive)

    def loop(body, start):
        if groups <= 4:
            for i in range(groups):
                start = body(i, start)
            return start
        return lax.fori_loop(0, groups, body, start)

    top = loop(lambda i, t: jnp.maximum(t, lse_all[i]), jnp.full((1, KV_HEADS * block), NEGATIVE_FILL, jnp.float32))

    def merge(i, carry):
        total, acc = carry
        share = jnp.exp2(lse_all[i] - top)
        return total + share, acc + share * part_all[i].astype(jnp.float32)

    total, acc = loop(
        merge,
        (jnp.zeros((1, KV_HEADS * block), jnp.float32), jnp.zeros((HEAD_DIM, KV_HEADS * block), jnp.float32)),
    )
    res[...] = (acc / total).T.astype(jnp.bfloat16).reshape(KV_HEADS, block, HEAD_DIM)

    f_copies = []
    for i, (m, target) in enumerate(zip(mates, mate_ids)):
        f_copies.append(copy(res.at[m], fin.at[member], f_send.at[i], f_recv.at[member], target))
        f_copies[-1].start()
    fin[member] = res[member]
    for m, target in zip(mates, mate_ids):
        copy(fin.at[m], fin.at[m], f_send.at[0], f_recv.at[m], target).wait_recv()
    for s in range(KV_HEADS):
        done = fin[s].astype(jnp.float32)
        line = jnp.concatenate([done[h * rows:(h + 1) * rows] for h in range(per_group)], axis=1)
        width = per_group * HEAD_DIM
        out_ref[:, s * width:(s + 1) * width] = line.astype(jnp.bfloat16)

    for c in q_copies + m_copies + k_copies + v_copies + f_copies:
        c.wait_send()

    def drain(i):
        m_copy(i).wait_send()
        q_copy(i).wait_send()
        l_copy(i).wait_send()
        o_copy(i).wait_send()

    each(groups - 1, drain)


def shards(queries, key_cache, value_cache, tile_page, row_last):
    groups = lax.axis_size("blk") // KV_HEADS
    rows, width = queries.shape
    tokens = key_cache.shape[0]
    block = width // HEAD_DIM // KV_HEADS * rows
    bf16, f32 = jnp.bfloat16, jnp.float32
    dma = pltpu.SemaphoreType.DMA
    quad, far = dma((KV_HEADS,)), dma((groups,))
    return pl.pallas_call(
        functools.partial(kernel, groups),
        out_shape=jax.ShapeDtypeStruct((rows, width), bf16),
        in_specs=[pl.BlockSpec(memory_space=pl.ANY)] * 3
        + [pl.BlockSpec(memory_space=pltpu.VMEM), pl.BlockSpec(memory_space=pltpu.SMEM)],
        out_specs=pl.BlockSpec(memory_space=pltpu.VMEM),
        scratch_shapes=[
            pltpu.VMEM((rows, width), bf16),
            pltpu.VMEM(key_cache.shape, bf16),
            pltpu.VMEM(value_cache.shape, bf16),
            pltpu.VMEM((KV_HEADS, block, HEAD_DIM), bf16),
            pltpu.VMEM((KV_HEADS, HEAD_DIM, tokens), bf16),
            pltpu.VMEM((1, 128 + tokens), jnp.int32),
            pltpu.VMEM((groups, KV_HEADS, block, HEAD_DIM), bf16),
            pltpu.VMEM((KV_HEADS, tokens, HEAD_DIM), bf16),
            pltpu.VMEM((KV_HEADS, HEAD_DIM, tokens), bf16),
            pltpu.VMEM((KV_HEADS, 1, 128 + tokens), jnp.int32),
            pltpu.VMEM((groups, KV_HEADS, 1, 128), jnp.int32),
            pltpu.VMEM((KV_HEADS, tokens, HEAD_DIM), f32),
            pltpu.VMEM((groups, HEAD_DIM, KV_HEADS * block), bf16),
            pltpu.VMEM((groups, HEAD_DIM, KV_HEADS * block), bf16),
            pltpu.VMEM((groups, 1, KV_HEADS * block), f32),
            pltpu.VMEM((groups, 1, KV_HEADS * block), f32),
            pltpu.VMEM((KV_HEADS, block, HEAD_DIM), bf16),
            pltpu.VMEM((KV_HEADS, block, HEAD_DIM), bf16),
            dma((3,)),
            *([quad] * 8),
            *([far] * 8),
            *([quad] * 2),
        ],
        compiler_params=pltpu.CompilerParams(
            collective_id=0, has_side_effects=True, vmem_limit_bytes=40 * 1024 * 1024
        ),
        cost_estimate=pl.CostEstimate(flops=540_000_000, bytes_accessed=700_000, transcendentals=1_000_000),
    )(queries, key_cache, value_cache, tile_page.reshape(1, tokens), row_last)


def solution(mesh):
    placed = (
        P(("parts", "blk"), None),
        P(("parts", "blk"), None),
        P(("parts", "blk"), None),
        P(("parts", "blk")),
        P(("parts", "blk")),
    )
    return jax.shard_map(
        shards, mesh=mesh, in_specs=placed, out_specs=P(("parts", "blk"), None), check_vma=False
    )
```

```python
import functools
import math

import jax
import jax.numpy as jnp
from jax import lax
from jax.experimental import pallas as pl
from jax.experimental.pallas import tpu as pltpu
from jax.sharding import PartitionSpec as P

KV_HEADS = 4
HEAD_DIM = 128
NEGATIVE_FILL = -1e30
LOG2E = math.log2(math.e)
MESH = pl.DeviceIdType.MESH


def each(count, body):
    if count <= 15:
        for i in range(count):
            body(i)
    else:
        lax.fori_loop(0, count, lambda i, c: (body(i), c)[1], 0)


def kernel(
    groups, q_hbm, k_hbm, v_hbm, page_hbm, last_hbm, out_ref,
    q_in, last_in, q_pack, last_mine, q_all, k_all, v_all, v_turned, page_all, last_all, page_col,
    part_mine, part_all, lse_mine, lse_all,
    in_sem, own_sem, q_send, q_recv, qz_send, k_send, k_recv, v_send, v_recv,
    page_send, page_recv, last_send, last_recv, o_send, o_recv, l_send, l_recv,
):
    part, me = lax.axis_index("parts"), lax.axis_index("blk")
    member, group = lax.rem(me, KV_HEADS), lax.div(me, KV_HEADS)
    blocks = groups * KV_HEADS
    rows = q_in.shape[0]
    heads = q_in.shape[1] // HEAD_DIM
    tokens = k_all.shape[1]
    per_group = heads // KV_HEADS
    block = per_group * rows

    twin = member + 1 - 2 * lax.rem(member, 2)
    across = [lax.rem(member + 2, KV_HEADS), lax.rem(twin + 2, KV_HEADS)]
    mates = across + [twin]
    mate_ids = [group * KV_HEADS + m for m in mates]
    order = sorted(range(1, groups), key=lambda s: -min(s, groups - s))

    def peer(i):
        if groups <= 4:
            return lax.rem(group + order[i], groups)
        return lax.rem(group + 1 + i, groups)

    def copy(src, dst, send, recv, target):
        return pltpu.make_async_remote_copy(
            src_ref=src, dst_ref=dst, send_sem=send, recv_sem=recv,
            device_id=(part, target), device_id_type=MESH,
        )

    own = pl.ds(pl.multiple_of(member * HEAD_DIM, HEAD_DIM), HEAD_DIM)
    load_q = pltpu.make_async_copy(q_hbm, q_in, in_sem.at[0])
    load_last = pltpu.make_async_copy(last_hbm, last_in, in_sem.at[1])
    load_k = pltpu.make_async_copy(k_hbm.at[:, own], k_all.at[member], own_sem.at[0])
    load_v = pltpu.make_async_copy(v_hbm.at[:, own], v_all.at[member], own_sem.at[1])
    load_page = pltpu.make_async_copy(page_hbm, page_all.at[member], own_sem.at[2])
    load_q.start()
    load_last.start()

    barrier = pltpu.get_barrier_semaphore()

    def others(body):
        each(blocks - 1, lambda i: body(lax.rem(me + 1 + i, blocks)))

    def greet(target):
        pl.semaphore_signal(barrier, inc=1, device_id=(part, target), device_id_type=MESH)

    others(greet)
    load_k.start()
    load_v.start()
    load_page.start()

    load_q.wait()
    wide = q_in[...].astype(jnp.float32)
    stacked = jnp.concatenate(
        [wide[:, h * HEAD_DIM:(h + 1) * HEAD_DIM] for h in range(heads)], axis=0
    )
    q_pack[...] = stacked.astype(jnp.bfloat16).reshape(KV_HEADS, block, HEAD_DIM)
    q_all[group, member] = q_pack[member]

    load_last.wait()
    lane = lax.broadcasted_iota(jnp.int32, (1, 128), 1)
    pattern = jnp.zeros((1, 128), jnp.int32)
    for r in range(rows):
        pattern = jnp.where(lax.rem(lane, rows) == r, last_in[r], pattern)
    last_mine[...] = pattern
    last_all[me] = pattern

    pl.semaphore_wait(barrier, blocks - 1)

    q_copies = []
    for i, (m, target) in enumerate(zip(mates, mate_ids)):
        q_copies.append(copy(q_pack.at[m], q_all.at[group, member], q_send.at[i], q_recv.at[me], target))
        q_copies[-1].start()

    def direct(i, k):
        m = (member, twin)[k]
        return copy(
            q_pack.at[m], q_all.at[group, member], qz_send.at[peer(i), k], q_recv.at[me],
            peer(i) * KV_HEADS + m,
        )

    def relay(i, k):
        m = across[k]
        return copy(
            q_all.at[group, m], q_all.at[group, m], qz_send.at[peer(i), 2 + k],
            q_recv.at[group * KV_HEADS + m], peer(i) * KV_HEADS + member,
        )

    def send_direct(i):
        direct(i, 0).start()
        direct(i, 1).start()

    each(groups - 1, send_direct)

    kv_copies = []
    for i, (m, target) in enumerate(zip(mates, mate_ids)):
        columns = pl.ds(pl.multiple_of(m * HEAD_DIM, HEAD_DIM), HEAD_DIM)
        kv_copies.append(copy(k_hbm.at[:, columns], k_all.at[member], k_send.at[i], k_recv.at[member], target))
        kv_copies[-1].start()

    def q_wait(index):
        g, m = lax.div(index, KV_HEADS), lax.rem(index, KV_HEADS)
        copy(q_all.at[g, m], q_all.at[g, m], q_send.at[0], q_recv.at[index], mate_ids[0]).wait_recv()

    q_wait(mate_ids[0])
    q_wait(mate_ids[1])

    def send_relay(i):
        relay(i, 0).start()
        relay(i, 1).start()

    each(groups - 1, send_relay)

    for i, (m, target) in enumerate(zip(mates, mate_ids)):
        columns = pl.ds(pl.multiple_of(m * HEAD_DIM, HEAD_DIM), HEAD_DIM)
        copy(page_hbm, page_all.at[member], page_send, page_recv, target).start()
        kv_copies.append(copy(v_hbm.at[:, columns], v_all.at[member], v_send.at[i], v_recv.at[member], target))
        kv_copies[-1].start()
    others(lambda t: copy(last_mine, last_all.at[me], last_send, last_recv, t).start())

    few = pl.ds(0, KV_HEADS - 1)
    page_wait = copy(page_all.at[few], page_all.at[few], page_send, page_recv, mate_ids[0])
    rest = pl.ds(0, blocks - 1)
    last_wait = copy(last_all.at[rest], last_all.at[rest], last_send, last_recv, mate_ids[0])
    load_page.wait()
    page_wait.wait_recv()
    for s in range(KV_HEADS):
        pages = page_all[s].astype(jnp.float32)
        page_col[s] = jnp.broadcast_to(pages, (HEAD_DIM, tokens)).T

    factor = LOG2E / math.sqrt(HEAD_DIM)

    def weigh(which):
        per_row = 128 // block
        pieces = []
        for first in range(0, KV_HEADS, per_row):
            piece = last_all[which * KV_HEADS + first]
            for k in range(1, per_row):
                piece = jnp.where(lane < k * block, piece, last_all[which * KV_HEADS + first + k])
            pieces.append(piece)
        last_row = jnp.concatenate(pieces, axis=1).astype(jnp.float32)
        queries = q_all[which].reshape(KV_HEADS * block, HEAD_DIM)
        masked = []
        for s in range(KV_HEADS):
            scores = lax.dot_general(
                k_all[s], queries, (((1,), (1,)), ((), ())), preferred_element_type=jnp.float32
            )
            pages = jnp.concatenate([page_col[s]] * len(pieces), axis=1)
            masked.append(jnp.where(pages <= last_row, scores, NEGATIVE_FILL))
        top = functools.reduce(jnp.maximum, [jnp.max(x, axis=0, keepdims=True) for x in masked])
        total = jnp.zeros_like(top)
        rounded = []
        for s in range(KV_HEADS):
            weights = jnp.exp2((masked[s] - top) * factor)
            total = total + jnp.sum(weights, axis=0, keepdims=True)
            rounded.append(weights.astype(jnp.bfloat16))
        return rounded, total, top * factor + jnp.log(total) * LOG2E

    def attend(weighed):
        rounded, total, lse = weighed
        out = jnp.zeros((HEAD_DIM, KV_HEADS * block), jnp.float32)
        for s in range(KV_HEADS):
            out = out + jnp.dot(v_turned[s], rounded[s], preferred_element_type=jnp.float32)
        out = (out / total).T.astype(jnp.bfloat16).reshape(KV_HEADS, block, HEAD_DIM)
        return out, lse

    def far_weigh(i):
        for m in range(KV_HEADS):
            q_wait(peer(i) * KV_HEADS + m)
        return weigh(peer(i))

    def send_out(index):
        copy(lse_mine.at[index], lse_all.at[me], l_send, l_recv, index).start()
        copy(part_mine.at[index], part_all.at[me], o_send, o_recv, index).start()

    def far_attend(i, weighed):
        out, lse = attend(weighed)
        base = peer(i) * KV_HEADS
        part_mine[pl.ds(base, KV_HEADS)] = out
        for m in range(KV_HEADS):
            first = m * block // 128 * 128
            lse_mine[base + m] = lse[:, first:first + 128]
        for m in range(KV_HEADS):
            send_out(base + m)

    q_wait(mate_ids[2])
    load_k.wait()
    for m, target in zip(mates, mate_ids):
        copy(k_all.at[m], k_all.at[m], k_send.at[0], k_recv.at[m], target).wait_recv()
    last_wait.wait_recv()
    own_weighed = weigh(group)
    first_weighed = far_weigh(0)

    load_v.wait()
    for m, target in zip(mates, mate_ids):
        copy(v_all.at[m], v_all.at[m], v_send.at[0], v_recv.at[m], target).wait_recv()
    for s in range(KV_HEADS):
        v_turned[s] = v_all[s].astype(jnp.float32).T.astype(jnp.bfloat16)

    far_attend(0, first_weighed)
    each(groups - 2, lambda i: far_attend(i + 1, far_weigh(i + 1)))
    out, lse = attend(own_weighed)
    base = group * KV_HEADS
    part_mine[pl.ds(base, KV_HEADS)] = out
    for m in range(KV_HEADS):
        first = m * block // 128 * 128
        lse_mine[base + m] = lse[:, first:first + 128]
    for target in mate_ids:
        send_out(target)
    part_all[me] = part_mine[me]
    lse_all[me] = lse_mine[me]

    lse_wait = copy(lse_all.at[rest], lse_all.at[rest], l_send, l_recv, mate_ids[0])
    out_wait = copy(part_all.at[rest], part_all.at[rest], o_send, o_recv, mate_ids[0])
    lse_wait.wait_recv()
    shares = [None] * blocks
    for m in range(KV_HEADS):
        found = [lse_all[g * KV_HEADS + m] for g in range(groups)]
        top = functools.reduce(jnp.maximum, found)
        found = [jnp.exp2(x - top) for x in found]
        total = functools.reduce(jnp.add, found)
        for g in range(groups):
            shares[g * KV_HEADS + m] = found[g] / total
    if blocks < 128:
        shares.append(jnp.zeros((128 - blocks, 128), jnp.float32))
    turned = jnp.concatenate(shares, axis=0).T
    place = lax.rem(member, 128 // block)
    columns = turned[:block]
    for k in range(1, 128 // block):
        columns = jnp.where(place == k, turned[k * block:(k + 1) * block], columns)

    out_wait.wait_recv()
    for m in range(KV_HEADS):
        done = jnp.zeros((block, HEAD_DIM), jnp.float32)
        for g in range(groups):
            source = g * KV_HEADS + m
            done = done + columns[:, source:source + 1] * part_all[source].astype(jnp.float32)
        line = jnp.concatenate([done[h * rows:(h + 1) * rows] for h in range(per_group)], axis=1)
        width = per_group * HEAD_DIM
        out_ref[:, m * width:(m + 1) * width] = line.astype(jnp.bfloat16)

    for c in q_copies + kv_copies:
        c.wait_send()

    def drain(i):
        for k in range(2):
            direct(i, k).wait_send()
            relay(i, k).wait_send()

    each(groups - 1, drain)
    page_wait.wait_send()
    last_wait.wait_send()
    lse_wait.wait_send()
    out_wait.wait_send()


def shards(queries, key_cache, value_cache, tile_page, row_last):
    groups = lax.axis_size("blk") // KV_HEADS
    blocks = lax.axis_size("blk")
    rows, width = queries.shape
    tokens = key_cache.shape[0]
    block = width // HEAD_DIM // KV_HEADS * rows
    bf16, f32 = jnp.bfloat16, jnp.float32
    dma = pltpu.SemaphoreType.DMA
    quad, one = dma((KV_HEADS,)), dma
    return pl.pallas_call(
        functools.partial(kernel, groups),
        out_shape=jax.ShapeDtypeStruct((rows, width), bf16),
        in_specs=[pl.BlockSpec(memory_space=pltpu.HBM)] * 5,
        out_specs=pl.BlockSpec(memory_space=pltpu.VMEM),
        scratch_shapes=[
            pltpu.VMEM((rows, width), bf16),
            pltpu.SMEM((rows,), jnp.int32),
            pltpu.VMEM((KV_HEADS, block, HEAD_DIM), bf16),
            pltpu.VMEM((1, 128), jnp.int32),
            pltpu.VMEM((groups, KV_HEADS, block, HEAD_DIM), bf16),
            pltpu.VMEM((KV_HEADS, tokens, HEAD_DIM), bf16),
            pltpu.VMEM((KV_HEADS, tokens, HEAD_DIM), bf16),
            pltpu.VMEM((KV_HEADS, HEAD_DIM, tokens), bf16),
            pltpu.VMEM((KV_HEADS, 1, tokens), jnp.int32),
            pltpu.VMEM((blocks, 1, 128), jnp.int32),
            pltpu.VMEM((KV_HEADS, tokens, HEAD_DIM), f32),
            pltpu.VMEM((blocks, block, HEAD_DIM), bf16),
            pltpu.VMEM((blocks, block, HEAD_DIM), bf16),
            pltpu.VMEM((blocks, 1, 128), f32),
            pltpu.VMEM((blocks, 1, 128), f32),
            dma((2,)), dma((3,)),
            quad, dma((blocks,)), dma((groups, 4)), quad, quad, quad, quad,
            one, one, one, one, one, one, one, one,
        ],
        compiler_params=pltpu.CompilerParams(
            collective_id=0, has_side_effects=True, vmem_limit_bytes=60 * 1024 * 1024
        ),
        cost_estimate=pl.CostEstimate(flops=540_000_000, bytes_accessed=700_000, transcendentals=1_000_000),
    )(queries, key_cache, value_cache, tile_page.reshape(1, tokens), row_last)


def solution(mesh):
    placed = (
        P(("parts", "blk"), None),
        P(("parts", "blk"), None),
        P(("parts", "blk"), None),
        P(("parts", "blk")),
        P(("parts", "blk")),
    )
    return jax.shard_map(
        shards, mesh=mesh, in_specs=placed, out_specs=P(("parts", "blk"), None), check_vma=False
    )
```

```python
import functools
import math

import jax
import jax.numpy as jnp
from jax import lax
from jax.experimental import pallas as pl
from jax.experimental.pallas import tpu as pltpu
from jax.sharding import PartitionSpec as P

KV_HEADS = 4
HEAD_DIM = 128
NEGATIVE_FILL = -1e30
LOG2E = math.log2(math.e)
MESH = pl.DeviceIdType.MESH
AHEAD = 2


def each(count, body):
    if count <= 15:
        for i in range(count):
            body(i)
    else:
        lax.fori_loop(0, count, lambda i, c: (body(i), c)[1], 0)


def kernel(
    groups, q_hbm, k_hbm, v_hbm, page_hbm, last_hbm, out_ref,
    q_in, v_in, last_in, q_pack, last_mine, q_all, k_all, v_mine, v_all, page_all, last_all, page_col,
    part_mine, part_all, lse_mine, lse_all, share_ref,
    in_sem, own_sem, q_send, q_recv, qz_send, k_send, k_recv, v_send, v_recv,
    page_send, page_recv, last_send, last_recv, o_send, o_recv, l_send, l_recv,
):
    part, me = lax.axis_index("parts"), lax.axis_index("blk")
    member, group = lax.rem(me, KV_HEADS), lax.div(me, KV_HEADS)
    blocks = groups * KV_HEADS
    rows = q_in.shape[0]
    heads = q_in.shape[1] // HEAD_DIM
    tokens = k_all.shape[1]
    per_group = heads // KV_HEADS
    block = per_group * rows

    twin = member + 1 - 2 * lax.rem(member, 2)
    across = [lax.rem(member + 2, KV_HEADS), lax.rem(twin + 2, KV_HEADS)]
    mates = across + [twin]
    mate_ids = [group * KV_HEADS + m for m in mates]
    order = sorted(range(1, groups), key=lambda s: -min(s, groups - s))

    def peer(i):
        if groups <= 4:
            return lax.rem(group + order[i], groups)
        return lax.rem(group + 1 + i, groups)

    def source_at(i):
        if groups <= 4:
            return lax.rem(group + groups - order[i], groups)
        return lax.rem(group + groups - 1 - i, groups)

    def copy(src, dst, send, recv, target):
        return pltpu.make_async_remote_copy(
            src_ref=src, dst_ref=dst, send_sem=send, recv_sem=recv,
            device_id=(part, target), device_id_type=MESH,
        )

    own = pl.ds(pl.multiple_of(member * HEAD_DIM, HEAD_DIM), HEAD_DIM)
    load_q = pltpu.make_async_copy(q_hbm, q_in, in_sem.at[0])
    load_last = pltpu.make_async_copy(last_hbm, last_in, in_sem.at[1])
    load_k = pltpu.make_async_copy(k_hbm.at[:, own], k_all.at[member], own_sem.at[0])
    load_v = pltpu.make_async_copy(v_hbm, v_in, own_sem.at[1])
    load_page = pltpu.make_async_copy(page_hbm, page_all.at[member], own_sem.at[2])
    load_q.start()
    load_last.start()

    barrier = pltpu.get_barrier_semaphore()

    def others(body):
        each(blocks - 1, lambda i: body(lax.rem(me + 1 + i, blocks)))

    def greet(target):
        pl.semaphore_signal(barrier, inc=1, device_id=(part, target), device_id_type=MESH)

    others(greet)
    load_k.start()
    load_v.start()
    load_page.start()

    load_q.wait()
    wide = q_in[...].astype(jnp.float32)
    stacked = jnp.concatenate(
        [wide[:, h * HEAD_DIM:(h + 1) * HEAD_DIM] for h in range(heads)], axis=0
    )
    q_pack[...] = stacked.astype(jnp.bfloat16).reshape(KV_HEADS, block, HEAD_DIM)
    q_all[group, member] = q_pack[member]

    load_last.wait()
    lane = lax.broadcasted_iota(jnp.int32, (1, 128), 1)
    pattern = jnp.zeros((1, 128), jnp.int32)
    for r in range(rows):
        pattern = jnp.where(lax.rem(lane, rows) == r, last_in[r], pattern)
    last_mine[...] = pattern
    last_all[me] = pattern

    pl.semaphore_wait(barrier, blocks - 1)

    q_copies = []
    for i, (m, target) in enumerate(zip(mates, mate_ids)):
        q_copies.append(copy(q_pack.at[m], q_all.at[group, member], q_send.at[i], q_recv.at[me], target))
        q_copies[-1].start()

    def direct(i, k):
        m = (member, twin)[k]
        return copy(
            q_pack.at[m], q_all.at[group, member], qz_send.at[peer(i), k], q_recv.at[me],
            peer(i) * KV_HEADS + m,
        )

    def relay(i, k):
        m = across[k]
        return copy(
            q_all.at[group, m], q_all.at[group, m], qz_send.at[peer(i), 2 + k],
            q_recv.at[group * KV_HEADS + m], peer(i) * KV_HEADS + member,
        )

    def send_direct(i):
        direct(i, 0).start()
        direct(i, 1).start()

    each(groups - 1, send_direct)

    kv_copies = []
    for i, (m, target) in enumerate(zip(mates, mate_ids)):
        columns = pl.ds(pl.multiple_of(m * HEAD_DIM, HEAD_DIM), HEAD_DIM)
        kv_copies.append(copy(k_hbm.at[:, columns], k_all.at[member], k_send.at[i], k_recv.at[member], target))
        kv_copies[-1].start()

    def q_wait(index):
        g, m = lax.div(index, KV_HEADS), lax.rem(index, KV_HEADS)
        copy(q_all.at[g, m], q_all.at[g, m], q_send.at[0], q_recv.at[index], mate_ids[0]).wait_recv()

    load_v.wait()
    v_mine[...] = (
        v_in[...].astype(jnp.float32).T.astype(jnp.bfloat16).reshape(KV_HEADS, HEAD_DIM, tokens)
    )
    for i, (m, target) in enumerate(zip(mates, mate_ids)):
        kv_copies.append(copy(v_mine.at[m], v_all.at[member], v_send.at[i], v_recv.at[member], target))
        kv_copies[-1].start()
    v_all[member] = v_mine[member]

    q_wait(mate_ids[0])
    q_wait(mate_ids[1])

    def send_relay(i):
        relay(i, 0).start()
        relay(i, 1).start()

    each(groups - 1, send_relay)

    for target in mate_ids:
        copy(page_hbm, page_all.at[member], page_send, page_recv, target).start()
    others(lambda t: copy(last_mine, last_all.at[me], last_send, last_recv, t).start())

    few = pl.ds(0, KV_HEADS - 1)
    page_wait = copy(page_all.at[few], page_all.at[few], page_send, page_recv, mate_ids[0])
    rest = pl.ds(0, blocks - 1)
    last_wait = copy(last_all.at[rest], last_all.at[rest], last_send, last_recv, mate_ids[0])
    load_page.wait()
    page_wait.wait_recv()
    for s in range(KV_HEADS):
        pages = page_all[s].astype(jnp.float32)
        page_col[s] = jnp.broadcast_to(pages, (HEAD_DIM, tokens)).T

    factor = LOG2E / math.sqrt(HEAD_DIM)

    def weigh(which):
        per_row = 128 // block
        pieces = []
        for first in range(0, KV_HEADS, per_row):
            piece = last_all[which * KV_HEADS + first]
            for k in range(1, per_row):
                piece = jnp.where(lane < k * block, piece, last_all[which * KV_HEADS + first + k])
            pieces.append(piece)
        last_row = jnp.concatenate(pieces, axis=1).astype(jnp.float32)
        queries = q_all[which].reshape(KV_HEADS * block, HEAD_DIM)
        masked = []
        for s in range(KV_HEADS):
            scores = lax.dot_general(
                k_all[s], queries, (((1,), (1,)), ((), ())), preferred_element_type=jnp.float32
            )
            pages = jnp.concatenate([page_col[s]] * len(pieces), axis=1)
            masked.append(jnp.where(pages <= last_row, scores, NEGATIVE_FILL))
        top = functools.reduce(jnp.maximum, [jnp.max(x, axis=0, keepdims=True) for x in masked])
        total = jnp.zeros_like(top)
        rounded = []
        for s in range(KV_HEADS):
            weights = jnp.exp2((masked[s] - top) * factor)
            total = total + jnp.sum(weights, axis=0, keepdims=True)
            rounded.append(weights.astype(jnp.bfloat16))
        return rounded, total, top * factor + jnp.log(total) * LOG2E

    def attend(weighed):
        rounded, total = weighed
        out = jnp.zeros((HEAD_DIM, KV_HEADS * block), jnp.float32)
        for s in range(KV_HEADS):
            out = out + jnp.dot(v_all[s], rounded[s], preferred_element_type=jnp.float32)
        out = (out * (1.0 / total)).T.astype(jnp.bfloat16).reshape(KV_HEADS, block, HEAD_DIM)
        return out

    def share_lse(which, lse):
        base = which * KV_HEADS
        for m in range(KV_HEADS):
            first = m * block // 128 * 128
            lse_mine[base + m] = lse[:, first:first + 128]

    def far_weigh(i):
        base = peer(i) * KV_HEADS
        for m in range(KV_HEADS):
            q_wait(base + m)
        rounded, total, lse = weigh(peer(i))
        share_lse(peer(i), lse)
        for m in range(KV_HEADS):
            copy(lse_mine.at[base + m], lse_all.at[me], l_send, l_recv, base + m).start()
        return rounded, total

    def send_out(index):
        copy(part_mine.at[index], part_all.at[me], o_send, o_recv.at[group], index).start()

    def far_attend(i, weighed):
        base = peer(i) * KV_HEADS
        part_mine[pl.ds(base, KV_HEADS)] = attend(weighed)
        for m in range(KV_HEADS):
            send_out(base + m)

    q_wait(mate_ids[2])
    load_k.wait()
    for m, target in zip(mates, mate_ids):
        copy(k_all.at[m], k_all.at[m], k_send.at[0], k_recv.at[m], target).wait_recv()
    last_wait.wait_recv()
    rounded, total, lse = weigh(group)
    own_weighed = rounded, total
    share_lse(group, lse)
    for target in mate_ids:
        copy(lse_mine.at[target], lse_all.at[me], l_send, l_recv, target).start()
    lse_all[me] = lse_mine[me]
    ahead = [far_weigh(i) for i in range(min(AHEAD, groups - 1))]

    for m, target in zip(mates, mate_ids):
        copy(v_all.at[m], v_all.at[m], v_send.at[0], v_recv.at[m], target).wait_recv()

    for i, weighed in enumerate(ahead):
        far_attend(i, weighed)
    each(groups - 1 - len(ahead), lambda i: far_attend(i + len(ahead), far_weigh(i + len(ahead))))
    base = group * KV_HEADS
    part_mine[pl.ds(base, KV_HEADS)] = attend(own_weighed)
    for target in mate_ids:
        send_out(target)
    part_all[me] = part_mine[me]

    lse_wait = copy(lse_all.at[rest], lse_all.at[rest], l_send, l_recv, mate_ids[0])
    lse_wait.wait_recv()
    shares = [None] * blocks
    for m in range(KV_HEADS):
        found = [lse_all[g * KV_HEADS + m] for g in range(groups)]
        top = functools.reduce(jnp.maximum, found)
        found = [jnp.exp2(x - top) for x in found]
        total = functools.reduce(jnp.add, found)
        for g in range(groups):
            shares[g * KV_HEADS + m] = found[g] / total
    if blocks < 128:
        shares.append(jnp.zeros((128 - blocks, 128), jnp.float32))
    turned = jnp.concatenate(shares, axis=0).T
    place = lax.rem(member, 128 // block)
    columns = turned[:block]
    for k in range(1, 128 // block):
        columns = jnp.where(place == k, turned[k * block:(k + 1) * block], columns)

    def out_wait(which, count):
        part_ref = part_all.at[pl.ds(0, count)]
        return copy(part_ref, part_ref, o_send, o_recv.at[which], mate_ids[0])

    width = per_group * HEAD_DIM

    def add_group(which, done):
        found = []
        for m in range(KV_HEADS):
            part_out = part_all[which * KV_HEADS + m].astype(jnp.float32)
            found.append(done[m] + share_ref[which * KV_HEADS + m] * part_out)
        return found

    for source in range(blocks):
        share_ref[source] = jnp.broadcast_to(columns[:, source:source + 1], (block, HEAD_DIM))
    done = [jnp.zeros((block, HEAD_DIM), jnp.float32)] * KV_HEADS
    out_wait(group, KV_HEADS - 1).wait_recv()
    done = add_group(group, done)
    if groups <= 4:
        for i in range(groups - 1):
            out_wait(source_at(i), KV_HEADS).wait_recv()
            done = add_group(source_at(i), done)
    else:
        def more(i, done):
            out_wait(source_at(i), KV_HEADS).wait_recv()
            return tuple(add_group(source_at(i), list(done)))

        done = lax.fori_loop(0, groups - 1, more, tuple(done))
    for m in range(KV_HEADS):
        line = jnp.concatenate([done[m][h * rows:(h + 1) * rows] for h in range(per_group)], axis=1)
        out_ref[:, m * width:(m + 1) * width] = line.astype(jnp.bfloat16)

    for c in q_copies + kv_copies:
        c.wait_send()

    def drain(i):
        for k in range(2):
            direct(i, k).wait_send()
            relay(i, k).wait_send()

    each(groups - 1, drain)
    page_wait.wait_send()
    last_wait.wait_send()
    lse_wait.wait_send()
    copy(part_all.at[rest], part_all.at[rest], o_send, o_recv.at[0], mate_ids[0]).wait_send()


def shards(queries, key_cache, value_cache, tile_page, row_last):
    groups = lax.axis_size("blk") // KV_HEADS
    blocks = lax.axis_size("blk")
    rows, width = queries.shape
    tokens = key_cache.shape[0]
    block = width // HEAD_DIM // KV_HEADS * rows
    bf16, f32 = jnp.bfloat16, jnp.float32
    dma = pltpu.SemaphoreType.DMA
    quad, one = dma((KV_HEADS,)), dma
    return pl.pallas_call(
        functools.partial(kernel, groups),
        out_shape=jax.ShapeDtypeStruct((rows, width), bf16),
        in_specs=[pl.BlockSpec(memory_space=pltpu.HBM)] * 5,
        out_specs=pl.BlockSpec(memory_space=pltpu.VMEM),
        scratch_shapes=[
            pltpu.VMEM((rows, width), bf16),
            pltpu.VMEM(value_cache.shape, bf16),
            pltpu.SMEM((rows,), jnp.int32),
            pltpu.VMEM((KV_HEADS, block, HEAD_DIM), bf16),
            pltpu.VMEM((1, 128), jnp.int32),
            pltpu.VMEM((groups, KV_HEADS, block, HEAD_DIM), bf16),
            pltpu.VMEM((KV_HEADS, tokens, HEAD_DIM), bf16),
            pltpu.VMEM((KV_HEADS, HEAD_DIM, tokens), bf16),
            pltpu.VMEM((KV_HEADS, HEAD_DIM, tokens), bf16),
            pltpu.VMEM((KV_HEADS, 1, tokens), jnp.int32),
            pltpu.VMEM((blocks, 1, 128), jnp.int32),
            pltpu.VMEM((KV_HEADS, tokens, HEAD_DIM), f32),
            pltpu.VMEM((blocks, block, HEAD_DIM), bf16),
            pltpu.VMEM((blocks, block, HEAD_DIM), bf16),
            pltpu.VMEM((blocks, 1, 128), f32),
            pltpu.VMEM((blocks, 1, 128), f32),
            pltpu.VMEM((blocks, block, HEAD_DIM), f32),
            dma((2,)), dma((3,)),
            quad, dma((blocks,)), dma((groups, 4)), quad, quad, quad, quad,
            one, one, one, one, one, dma((groups,)), one, one,
        ],
        compiler_params=pltpu.CompilerParams(
            collective_id=0, has_side_effects=True, vmem_limit_bytes=60 * 1024 * 1024
        ),
        cost_estimate=pl.CostEstimate(flops=540_000_000, bytes_accessed=700_000, transcendentals=1_000_000),
    )(queries, key_cache, value_cache, tile_page.reshape(1, tokens), row_last)


def solution(mesh):
    placed = (
        P(("parts", "blk"), None),
        P(("parts", "blk"), None),
        P(("parts", "blk"), None),
        P(("parts", "blk")),
        P(("parts", "blk")),
    )
    return jax.shard_map(
        shards, mesh=mesh, in_specs=placed, out_specs=P(("parts", "blk"), None), check_vma=False
    )
```

```python
import functools
import math

import jax
import jax.numpy as jnp
from jax import lax
from jax.experimental import pallas as pl
from jax.experimental.pallas import tpu as pltpu
from jax.sharding import PartitionSpec as P

KV_HEADS = 4
HEAD_DIM = 128
NEGATIVE_FILL = -1e30
LOG2E = math.log2(math.e)
MESH = pl.DeviceIdType.MESH
AHEAD = 2


def each(count, body):
    if count <= 15:
        for i in range(count):
            body(i)
    else:
        lax.fori_loop(0, count, lambda i, c: (body(i), c)[1], 0)


def kernel(
    groups, q_hbm, k_hbm, v_hbm, page_hbm, last_hbm, out_ref,
    q_in, v_in, last_in, q_pack, last_mine, q_all, k_all, v_mine, v_all, page_all, last_all, page_col,
    part_mine, part_all, lse_mine, lse_all, share_ref,
    in_sem, own_sem, q_send, q_recv, qz_send, k_send, k_recv, v_send, v_recv,
    page_send, page_recv, last_send, last_recv, o_send, o_recv, l_send, l_recv,
):
    part, me = lax.axis_index("parts"), lax.axis_index("blk")
    member, group = lax.rem(me, KV_HEADS), lax.div(me, KV_HEADS)
    blocks = groups * KV_HEADS
    rows = q_in.shape[0]
    heads = q_in.shape[1] // HEAD_DIM
    tokens = k_all.shape[1]
    per_group = heads // KV_HEADS
    block = per_group * rows

    twin = member + 1 - 2 * lax.rem(member, 2)
    across = [lax.rem(member + 2, KV_HEADS), lax.rem(twin + 2, KV_HEADS)]
    mates = across + [twin]
    mate_ids = [group * KV_HEADS + m for m in mates]

    def peer(i):
        if groups == 4:
            return (
                lax.rem(group + 2, 4),
                groups - 1 - group,
                group + 1 - 2 * lax.rem(group, 2),
            )[i]
        return lax.rem(group + 1 + i, groups)

    def source_at(i):
        if groups == 4:
            return peer(i)
        return lax.rem(group + groups - 1 - i, groups)

    def copy(src, dst, send, recv, target):
        return pltpu.make_async_remote_copy(
            src_ref=src, dst_ref=dst, send_sem=send, recv_sem=recv,
            device_id=(part, target), device_id_type=MESH,
        )

    own = pl.ds(pl.multiple_of(member * HEAD_DIM, HEAD_DIM), HEAD_DIM)
    load_q = pltpu.make_async_copy(q_hbm, q_in, in_sem.at[0])
    load_last = pltpu.make_async_copy(last_hbm, last_in, in_sem.at[1])
    load_k = pltpu.make_async_copy(k_hbm.at[:, own], k_all.at[member], own_sem.at[0])
    load_v = pltpu.make_async_copy(v_hbm, v_in, own_sem.at[1])
    load_page = pltpu.make_async_copy(page_hbm, page_all.at[member], own_sem.at[2])
    load_q.start()
    load_last.start()

    barrier = pltpu.get_barrier_semaphore()

    def others(body):
        each(blocks - 1, lambda i: body(lax.rem(me + 1 + i, blocks)))

    def greet(target):
        pl.semaphore_signal(barrier, inc=1, device_id=(part, target), device_id_type=MESH)

    others(greet)
    load_k.start()
    load_v.start()
    load_page.start()

    load_q.wait()
    wide = q_in[...].astype(jnp.float32)
    stacked = jnp.concatenate(
        [wide[:, h * HEAD_DIM:(h + 1) * HEAD_DIM] for h in range(heads)], axis=0
    )
    q_pack[...] = stacked.astype(jnp.bfloat16).reshape(KV_HEADS, block, HEAD_DIM)
    q_all[group, member] = q_pack[member]

    load_last.wait()
    lane = lax.broadcasted_iota(jnp.int32, (1, 128), 1)
    pattern = jnp.zeros((1, 128), jnp.int32)
    for r in range(rows):
        pattern = jnp.where(lax.rem(lane, rows) == r, last_in[r], pattern)
    last_mine[...] = pattern
    last_all[me] = pattern

    pl.semaphore_wait(barrier, blocks - 1)

    def direct(i, k):
        m = (member, twin)[k]
        return copy(
            q_pack.at[m], q_all.at[group, member], qz_send.at[peer(i), k], q_recv.at[me],
            peer(i) * KV_HEADS + m,
        )

    def relay(i, k):
        m = across[k]
        return copy(
            q_all.at[group, m], q_all.at[group, m], qz_send.at[peer(i), 2 + k],
            q_recv.at[group * KV_HEADS + m], peer(i) * KV_HEADS + member,
        )

    def send_direct(i):
        direct(i, 0).start()
        direct(i, 1).start()

    q_copies, kv_copies = [], []

    def send_q(i):
        q_copies.append(copy(q_pack.at[mates[i]], q_all.at[group, member], q_send.at[i], q_recv.at[me], mate_ids[i]))
        q_copies[-1].start()

    def send_k(i):
        columns = pl.ds(pl.multiple_of(mates[i] * HEAD_DIM, HEAD_DIM), HEAD_DIM)
        kv_copies.append(copy(k_hbm.at[:, columns], k_all.at[member], k_send.at[i], k_recv.at[member], mate_ids[i]))
        kv_copies[-1].start()

    for send, i in ((send_q, 0), (send_q, 1), (send_k, 0), (send_k, 1)):
        send(i)
    each(groups - 1, send_direct)
    send_q(2)
    send_k(2)

    def q_wait(index):
        g, m = lax.div(index, KV_HEADS), lax.rem(index, KV_HEADS)
        copy(q_all.at[g, m], q_all.at[g, m], q_send.at[0], q_recv.at[index], mate_ids[0]).wait_recv()

    load_v.wait()
    v_mine[...] = (
        v_in[...].astype(jnp.float32).T.astype(jnp.bfloat16).reshape(KV_HEADS, HEAD_DIM, tokens)
    )
    for i, (m, target) in enumerate(zip(mates, mate_ids)):
        kv_copies.append(copy(v_mine.at[m], v_all.at[member], v_send.at[i], v_recv.at[member], target))
        kv_copies[-1].start()
    v_all[member] = v_mine[member]

    q_wait(mate_ids[0])
    q_wait(mate_ids[1])

    def send_relay(i):
        relay(i, 0).start()
        relay(i, 1).start()

    each(groups - 1, send_relay)

    for target in mate_ids:
        copy(page_hbm, page_all.at[member], page_send, page_recv, target).start()
    others(lambda t: copy(last_mine, last_all.at[me], last_send, last_recv, t).start())

    few = pl.ds(0, KV_HEADS - 1)
    page_wait = copy(page_all.at[few], page_all.at[few], page_send, page_recv, mate_ids[0])
    rest = pl.ds(0, blocks - 1)
    last_wait = copy(last_all.at[rest], last_all.at[rest], last_send, last_recv, mate_ids[0])
    load_page.wait()
    page_wait.wait_recv()
    for s in range(KV_HEADS):
        pages = page_all[s].astype(jnp.float32)
        page_col[s] = jnp.broadcast_to(pages, (HEAD_DIM, tokens)).T

    factor = LOG2E / math.sqrt(HEAD_DIM)

    def weigh(which):
        per_row = 128 // block
        pieces = []
        for first in range(0, KV_HEADS, per_row):
            piece = last_all[which * KV_HEADS + first]
            for k in range(1, per_row):
                piece = jnp.where(lane < k * block, piece, last_all[which * KV_HEADS + first + k])
            pieces.append(piece)
        last_row = jnp.concatenate(pieces, axis=1).astype(jnp.float32)
        queries = q_all[which].reshape(KV_HEADS * block, HEAD_DIM)
        masked = []
        for s in range(KV_HEADS):
            scores = lax.dot_general(
                k_all[s], queries, (((1,), (1,)), ((), ())), preferred_element_type=jnp.float32
            )
            pages = jnp.concatenate([page_col[s]] * len(pieces), axis=1)
            masked.append(jnp.where(pages <= last_row, scores, NEGATIVE_FILL))
        top = functools.reduce(jnp.maximum, [jnp.max(x, axis=0, keepdims=True) for x in masked])
        total = jnp.zeros_like(top)
        rounded = []
        for s in range(KV_HEADS):
            weights = jnp.exp2((masked[s] - top) * factor)
            total = total + jnp.sum(weights, axis=0, keepdims=True)
            rounded.append(weights.astype(jnp.bfloat16))
        return rounded, total, top * factor + jnp.log(total) * LOG2E

    def attend(weighed):
        rounded, total = weighed
        out = jnp.zeros((HEAD_DIM, KV_HEADS * block), jnp.float32)
        for s in range(KV_HEADS):
            out = out + jnp.dot(v_all[s], rounded[s], preferred_element_type=jnp.float32)
        out = (out * (1.0 / total)).T.astype(jnp.bfloat16).reshape(KV_HEADS, block, HEAD_DIM)
        return out

    def share_lse(which, lse):
        base = which * KV_HEADS
        for m in range(KV_HEADS):
            first = m * block // 128 * 128
            lse_mine[base + m] = lse[:, first:first + 128]

    def far_weigh(i):
        base = peer(i) * KV_HEADS
        for m in range(KV_HEADS):
            q_wait(base + m)
        rounded, total, lse = weigh(peer(i))
        share_lse(peer(i), lse)
        for m in range(KV_HEADS):
            copy(lse_mine.at[base + m], lse_all.at[me], l_send, l_recv, base + m).start()
        return rounded, total

    def send_out(index):
        copy(part_mine.at[index], part_all.at[me], o_send, o_recv.at[group], index).start()

    def far_attend(i, weighed):
        base = peer(i) * KV_HEADS
        part_mine[pl.ds(base, KV_HEADS)] = attend(weighed)
        for m in range(KV_HEADS):
            send_out(base + m)

    q_wait(mate_ids[2])
    load_k.wait()
    for m, target in zip(mates, mate_ids):
        copy(k_all.at[m], k_all.at[m], k_send.at[0], k_recv.at[m], target).wait_recv()
    last_wait.wait_recv()
    rounded, total, lse = weigh(group)
    own_weighed = rounded, total
    share_lse(group, lse)
    for target in mate_ids:
        copy(lse_mine.at[target], lse_all.at[me], l_send, l_recv, target).start()
    lse_all[me] = lse_mine[me]
    ahead = [far_weigh(i) for i in range(min(AHEAD, groups - 1))]

    for m, target in zip(mates, mate_ids):
        copy(v_all.at[m], v_all.at[m], v_send.at[0], v_recv.at[m], target).wait_recv()

    for i, weighed in enumerate(ahead):
        far_attend(i, weighed)
    each(groups - 1 - len(ahead), lambda i: far_attend(i + len(ahead), far_weigh(i + len(ahead))))
    base = group * KV_HEADS
    part_mine[pl.ds(base, KV_HEADS)] = attend(own_weighed)
    for target in mate_ids:
        send_out(target)
    part_all[me] = part_mine[me]

    lse_wait = copy(lse_all.at[rest], lse_all.at[rest], l_send, l_recv, mate_ids[0])
    lse_wait.wait_recv()
    shares = [None] * blocks
    for m in range(KV_HEADS):
        found = [lse_all[g * KV_HEADS + m] for g in range(groups)]
        top = functools.reduce(jnp.maximum, found)
        found = [jnp.exp2(x - top) for x in found]
        total = functools.reduce(jnp.add, found)
        for g in range(groups):
            shares[g * KV_HEADS + m] = found[g] / total
    if blocks < 128:
        shares.append(jnp.zeros((128 - blocks, 128), jnp.float32))
    turned = jnp.concatenate(shares, axis=0).T
    place = lax.rem(member, 128 // block)
    columns = turned[:block]
    for k in range(1, 128 // block):
        columns = jnp.where(place == k, turned[k * block:(k + 1) * block], columns)

    def out_wait(which, count):
        part_ref = part_all.at[pl.ds(0, count)]
        return copy(part_ref, part_ref, o_send, o_recv.at[which], mate_ids[0])

    width = per_group * HEAD_DIM

    def add_group(which, done):
        found = []
        for m in range(KV_HEADS):
            part_out = part_all[which * KV_HEADS + m].astype(jnp.float32)
            found.append(done[m] + share_ref[which * KV_HEADS + m] * part_out)
        return found

    for source in range(blocks):
        share_ref[source] = jnp.broadcast_to(columns[:, source:source + 1], (block, HEAD_DIM))
    done = [jnp.zeros((block, HEAD_DIM), jnp.float32)] * KV_HEADS
    out_wait(group, KV_HEADS - 1).wait_recv()
    done = add_group(group, done)
    if groups <= 4:
        for i in range(groups - 1):
            out_wait(source_at(i), KV_HEADS).wait_recv()
            done = add_group(source_at(i), done)
    else:
        def more(i, done):
            out_wait(source_at(i), KV_HEADS).wait_recv()
            return tuple(add_group(source_at(i), list(done)))

        done = lax.fori_loop(0, groups - 1, more, tuple(done))
    for m in range(KV_HEADS):
        line = jnp.concatenate([done[m][h * rows:(h + 1) * rows] for h in range(per_group)], axis=1)
        out_ref[:, m * width:(m + 1) * width] = line.astype(jnp.bfloat16)

    for c in q_copies + kv_copies:
        c.wait_send()

    def drain(i):
        for k in range(2):
            direct(i, k).wait_send()
            relay(i, k).wait_send()

    each(groups - 1, drain)
    page_wait.wait_send()
    last_wait.wait_send()
    lse_wait.wait_send()
    copy(part_all.at[rest], part_all.at[rest], o_send, o_recv.at[0], mate_ids[0]).wait_send()


def shards(queries, key_cache, value_cache, tile_page, row_last):
    groups = lax.axis_size("blk") // KV_HEADS
    blocks = lax.axis_size("blk")
    rows, width = queries.shape
    tokens = key_cache.shape[0]
    block = width // HEAD_DIM // KV_HEADS * rows
    bf16, f32 = jnp.bfloat16, jnp.float32
    dma = pltpu.SemaphoreType.DMA
    quad, one = dma((KV_HEADS,)), dma
    return pl.pallas_call(
        functools.partial(kernel, groups),
        out_shape=jax.ShapeDtypeStruct((rows, width), bf16),
        in_specs=[pl.BlockSpec(memory_space=pltpu.HBM)] * 5,
        out_specs=pl.BlockSpec(memory_space=pltpu.VMEM),
        scratch_shapes=[
            pltpu.VMEM((rows, width), bf16),
            pltpu.VMEM(value_cache.shape, bf16),
            pltpu.SMEM((rows,), jnp.int32),
            pltpu.VMEM((KV_HEADS, block, HEAD_DIM), bf16),
            pltpu.VMEM((1, 128), jnp.int32),
            pltpu.VMEM((groups, KV_HEADS, block, HEAD_DIM), bf16),
            pltpu.VMEM((KV_HEADS, tokens, HEAD_DIM), bf16),
            pltpu.VMEM((KV_HEADS, HEAD_DIM, tokens), bf16),
            pltpu.VMEM((KV_HEADS, HEAD_DIM, tokens), bf16),
            pltpu.VMEM((KV_HEADS, 1, tokens), jnp.int32),
            pltpu.VMEM((blocks, 1, 128), jnp.int32),
            pltpu.VMEM((KV_HEADS, tokens, HEAD_DIM), f32),
            pltpu.VMEM((blocks, block, HEAD_DIM), bf16),
            pltpu.VMEM((blocks, block, HEAD_DIM), bf16),
            pltpu.VMEM((blocks, 1, 128), f32),
            pltpu.VMEM((blocks, 1, 128), f32),
            pltpu.VMEM((blocks, block, HEAD_DIM), f32),
            dma((2,)), dma((3,)),
            quad, dma((blocks,)), dma((groups, 4)), quad, quad, quad, quad,
            one, one, one, one, one, dma((groups,)), one, one,
        ],
        compiler_params=pltpu.CompilerParams(
            collective_id=0, has_side_effects=True, vmem_limit_bytes=55104 * 1024
        ),
        cost_estimate=pl.CostEstimate(flops=540_000_000, bytes_accessed=700_000, transcendentals=1_000_000),
    )(queries, key_cache, value_cache, tile_page.reshape(1, tokens), row_last)


def solution(mesh):
    placed = (
        P(("parts", "blk"), None),
        P(("parts", "blk"), None),
        P(("parts", "blk"), None),
        P(("parts", "blk")),
        P(("parts", "blk")),
    )
    return jax.shard_map(
        shards, mesh=mesh, in_specs=placed, out_specs=P(("parts", "blk"), None), check_vma=False
    )
```

```python
import functools
import math

import jax
import jax.numpy as jnp
from jax import lax
from jax.experimental import pallas as pl
from jax.experimental.pallas import tpu as pltpu
from jax.sharding import PartitionSpec as P

KV_HEADS = 4
HEAD_DIM = 128
NEGATIVE_FILL = -1e30
LOG2E = math.log2(math.e)
MESH = pl.DeviceIdType.MESH
AHEAD = 1


def each(count, body):
    if count <= 15:
        for i in range(count):
            body(i)
    else:
        lax.fori_loop(0, count, lambda i, c: (body(i), c)[1], 0)


def kernel(
    groups, q_hbm, k_hbm, v_hbm, page_hbm, last_hbm, out_ref,
    q_in, v_in, last_in, q_pack, last_mine, q_all, k_all, v_mine, v_all, page_all, last_all, page_col,
    part_mine, part_all, lse_mine, lse_all, share_ref,
    in_sem, own_sem, q_send, q_recv, qz_send, k_send, k_recv, v_send, v_recv,
    page_send, page_recv, last_send, last_recv, o_send, o_recv, l_send, l_recv,
):
    part, me = lax.axis_index("parts"), lax.axis_index("blk")
    member, group = lax.rem(me, KV_HEADS), lax.div(me, KV_HEADS)
    blocks = groups * KV_HEADS
    rows = q_in.shape[0]
    heads = q_in.shape[1] // HEAD_DIM
    tokens = k_all.shape[1]
    per_group = heads // KV_HEADS
    block = per_group * rows

    twin = member + 1 - 2 * lax.rem(member, 2)
    across = [lax.rem(member + 2, KV_HEADS), lax.rem(twin + 2, KV_HEADS)]
    mates = across + [twin]
    mate_ids = [group * KV_HEADS + m for m in mates]

    def peer(i):
        if groups == 4:
            return (
                lax.rem(group + 2, 4),
                groups - 1 - group,
                group + 1 - 2 * lax.rem(group, 2),
            )[i]
        return lax.rem(group + 1 + i, groups)

    def source_at(i):
        if groups == 4:
            return peer(i)
        return lax.rem(group + groups - 1 - i, groups)

    def copy(src, dst, send, recv, target):
        return pltpu.make_async_remote_copy(
            src_ref=src, dst_ref=dst, send_sem=send, recv_sem=recv,
            device_id=(part, target), device_id_type=MESH,
        )

    own = pl.ds(pl.multiple_of(member * HEAD_DIM, HEAD_DIM), HEAD_DIM)
    load_q = pltpu.make_async_copy(q_hbm, q_in, in_sem.at[0])
    load_last = pltpu.make_async_copy(last_hbm, last_in, in_sem.at[1])
    load_k = pltpu.make_async_copy(k_hbm.at[:, own], k_all.at[member], own_sem.at[0])
    load_v = pltpu.make_async_copy(v_hbm, v_in, own_sem.at[1])
    load_page = pltpu.make_async_copy(page_hbm, page_all.at[member], own_sem.at[2])
    load_q.start()
    load_last.start()

    barrier = pltpu.get_barrier_semaphore()

    def others(body):
        each(blocks - 1, lambda i: body(lax.rem(me + 1 + i, blocks)))

    def greet(target):
        pl.semaphore_signal(barrier, inc=1, device_id=(part, target), device_id_type=MESH)

    others(greet)
    load_k.start()
    load_v.start()
    load_page.start()

    load_q.wait()
    wide = q_in[...].astype(jnp.float32)
    stacked = jnp.concatenate(
        [wide[:, h * HEAD_DIM:(h + 1) * HEAD_DIM] for h in range(heads)], axis=0
    )
    q_pack[...] = stacked.astype(jnp.bfloat16).reshape(KV_HEADS, block, HEAD_DIM)
    q_all[group, member] = q_pack[member]

    load_last.wait()
    lane = lax.broadcasted_iota(jnp.int32, (1, 128), 1)
    pattern = jnp.zeros((1, 128), jnp.int32)
    for r in range(rows):
        pattern = jnp.where(lax.rem(lane, rows) == r, last_in[r], pattern)
    last_mine[...] = pattern
    last_all[me] = pattern

    pl.semaphore_wait(barrier, blocks - 1)

    def direct(i, k):
        m = (member, twin)[k]
        return copy(
            q_pack.at[m], q_all.at[group, member], qz_send.at[peer(i), k], q_recv.at[me],
            peer(i) * KV_HEADS + m,
        )

    def relay(i, k):
        m = across[k]
        return copy(
            q_all.at[group, m], q_all.at[group, m], qz_send.at[peer(i), 2 + k],
            q_recv.at[group * KV_HEADS + m], peer(i) * KV_HEADS + member,
        )

    def send_direct(i):
        direct(i, 0).start()
        direct(i, 1).start()

    q_copies, kv_copies = [], []

    def send_q(i):
        q_copies.append(copy(q_pack.at[mates[i]], q_all.at[group, member], q_send.at[i], q_recv.at[me], mate_ids[i]))
        q_copies[-1].start()

    def send_k(i):
        columns = pl.ds(pl.multiple_of(mates[i] * HEAD_DIM, HEAD_DIM), HEAD_DIM)
        kv_copies.append(copy(k_hbm.at[:, columns], k_all.at[member], k_send.at[i], k_recv.at[member], mate_ids[i]))
        kv_copies[-1].start()

    for send, i in ((send_q, 0), (send_q, 1), (send_k, 0), (send_k, 1)):
        send(i)
    each(groups - 1, send_direct)
    send_q(2)
    send_k(2)

    def q_wait(index):
        g, m = lax.div(index, KV_HEADS), lax.rem(index, KV_HEADS)
        copy(q_all.at[g, m], q_all.at[g, m], q_send.at[0], q_recv.at[index], mate_ids[0]).wait_recv()

    q_wait(mate_ids[0])
    q_wait(mate_ids[1])

    def send_relay(i):
        relay(i, 0).start()
        relay(i, 1).start()

    each(groups - 1, send_relay)

    load_v.wait()
    v_mine[...] = (
        v_in[...].astype(jnp.float32).T.astype(jnp.bfloat16).reshape(KV_HEADS, HEAD_DIM, tokens)
    )
    for i, (m, target) in enumerate(zip(mates, mate_ids)):
        kv_copies.append(copy(v_mine.at[m], v_all.at[member], v_send.at[i], v_recv.at[member], target))
        kv_copies[-1].start()
    v_all[member] = v_mine[member]

    for target in mate_ids:
        copy(page_hbm, page_all.at[member], page_send, page_recv, target).start()
    others(lambda t: copy(last_mine, last_all.at[me], last_send, last_recv, t).start())

    few = pl.ds(0, KV_HEADS - 1)
    page_wait = copy(page_all.at[few], page_all.at[few], page_send, page_recv, mate_ids[0])
    rest = pl.ds(0, blocks - 1)
    last_wait = copy(last_all.at[rest], last_all.at[rest], last_send, last_recv, mate_ids[0])
    load_page.wait()
    page_wait.wait_recv()
    for s in range(KV_HEADS):
        pages = page_all[s].astype(jnp.float32)
        page_col[s] = jnp.broadcast_to(pages, (HEAD_DIM, tokens)).T

    factor = LOG2E / math.sqrt(HEAD_DIM)

    def weigh(which):
        per_row = 128 // block
        pieces = []
        for first in range(0, KV_HEADS, per_row):
            piece = last_all[which * KV_HEADS + first]
            for k in range(1, per_row):
                piece = jnp.where(lane < k * block, piece, last_all[which * KV_HEADS + first + k])
            pieces.append(piece)
        last_row = jnp.concatenate(pieces, axis=1).astype(jnp.float32)
        queries = q_all[which].reshape(KV_HEADS * block, HEAD_DIM)
        masked = []
        for s in range(KV_HEADS):
            scores = lax.dot_general(
                k_all[s], queries, (((1,), (1,)), ((), ())), preferred_element_type=jnp.float32
            )
            pages = jnp.concatenate([page_col[s]] * len(pieces), axis=1)
            masked.append(jnp.where(pages <= last_row, scores, NEGATIVE_FILL))
        top = functools.reduce(jnp.maximum, [jnp.max(x, axis=0, keepdims=True) for x in masked])
        total = jnp.zeros_like(top)
        rounded = []
        for s in range(KV_HEADS):
            weights = jnp.exp2((masked[s] - top) * factor)
            total = total + jnp.sum(weights, axis=0, keepdims=True)
            rounded.append(weights.astype(jnp.bfloat16))
        return rounded, total, top * factor + jnp.log(total) * LOG2E

    def attend(weighed):
        rounded, total = weighed
        out = jnp.zeros((HEAD_DIM, KV_HEADS * block), jnp.float32)
        for s in range(KV_HEADS):
            out = out + jnp.dot(v_all[s], rounded[s], preferred_element_type=jnp.float32)
        out = (out * (1.0 / total)).T.astype(jnp.bfloat16).reshape(KV_HEADS, block, HEAD_DIM)
        return out

    def share_lse(which, lse):
        base = which * KV_HEADS
        for m in range(KV_HEADS):
            first = m * block // 128 * 128
            lse_mine[base + m] = lse[:, first:first + 128]

    def far_weigh(i):
        base = peer(i) * KV_HEADS
        for m in range(KV_HEADS):
            q_wait(base + m)
        rounded, total, lse = weigh(peer(i))
        share_lse(peer(i), lse)
        for m in range(KV_HEADS):
            copy(lse_mine.at[base + m], lse_all.at[me], l_send, l_recv, base + m).start()
        return rounded, total

    def send_out(index):
        copy(part_mine.at[index], part_all.at[me], o_send, o_recv.at[group], index).start()

    def far_attend(i, weighed):
        base = peer(i) * KV_HEADS
        part_mine[pl.ds(base, KV_HEADS)] = attend(weighed)
        for m in range(KV_HEADS):
            send_out(base + m)

    q_wait(mate_ids[2])
    load_k.wait()
    for m, target in zip(mates, mate_ids):
        copy(k_all.at[m], k_all.at[m], k_send.at[0], k_recv.at[m], target).wait_recv()
    last_wait.wait_recv()
    rounded, total, lse = weigh(group)
    own_weighed = rounded, total
    share_lse(group, lse)
    for target in mate_ids:
        copy(lse_mine.at[target], lse_all.at[me], l_send, l_recv, target).start()
    lse_all[me] = lse_mine[me]
    ahead = [far_weigh(i) for i in range(min(AHEAD, groups - 1))]

    for m, target in zip(mates, mate_ids):
        copy(v_all.at[m], v_all.at[m], v_send.at[0], v_recv.at[m], target).wait_recv()

    for i, weighed in enumerate(ahead):
        far_attend(i, weighed)
    each(groups - 1 - len(ahead), lambda i: far_attend(i + len(ahead), far_weigh(i + len(ahead))))
    base = group * KV_HEADS
    part_mine[pl.ds(base, KV_HEADS)] = attend(own_weighed)
    for target in mate_ids:
        send_out(target)
    part_all[me] = part_mine[me]

    lse_wait = copy(lse_all.at[rest], lse_all.at[rest], l_send, l_recv, mate_ids[0])
    lse_wait.wait_recv()
    shares = [None] * blocks
    for m in range(KV_HEADS):
        found = [lse_all[g * KV_HEADS + m] for g in range(groups)]
        top = functools.reduce(jnp.maximum, found)
        found = [jnp.exp2(x - top) for x in found]
        total = functools.reduce(jnp.add, found)
        for g in range(groups):
            shares[g * KV_HEADS + m] = found[g] / total
    if blocks < 128:
        shares.append(jnp.zeros((128 - blocks, 128), jnp.float32))
    turned = jnp.concatenate(shares, axis=0).T
    place = lax.rem(member, 128 // block)
    columns = turned[:block]
    for k in range(1, 128 // block):
        columns = jnp.where(place == k, turned[k * block:(k + 1) * block], columns)

    def out_wait(which, count):
        part_ref = part_all.at[pl.ds(0, count)]
        return copy(part_ref, part_ref, o_send, o_recv.at[which], mate_ids[0])

    width = per_group * HEAD_DIM

    def add_group(which, done):
        found = []
        for m in range(KV_HEADS):
            part_out = part_all[which * KV_HEADS + m].astype(jnp.float32)
            found.append(done[m] + share_ref[which * KV_HEADS + m] * part_out)
        return found

    for source in range(blocks):
        share_ref[source] = jnp.broadcast_to(columns[:, source:source + 1], (block, HEAD_DIM))
    done = [jnp.zeros((block, HEAD_DIM), jnp.float32)] * KV_HEADS
    out_wait(group, KV_HEADS - 1).wait_recv()
    done = add_group(group, done)
    if groups <= 4:
        for i in range(groups - 1):
            out_wait(source_at(i), KV_HEADS).wait_recv()
            done = add_group(source_at(i), done)
    else:
        def more(i, done):
            out_wait(source_at(i), KV_HEADS).wait_recv()
            return tuple(add_group(source_at(i), list(done)))

        done = lax.fori_loop(0, groups - 1, more, tuple(done))
    for m in range(KV_HEADS):
        line = jnp.concatenate([done[m][h * rows:(h + 1) * rows] for h in range(per_group)], axis=1)
        out_ref[:, m * width:(m + 1) * width] = line.astype(jnp.bfloat16)

    for c in q_copies + kv_copies:
        c.wait_send()

    def drain(i):
        for k in range(2):
            direct(i, k).wait_send()
            relay(i, k).wait_send()

    each(groups - 1, drain)
    page_wait.wait_send()
    last_wait.wait_send()
    lse_wait.wait_send()
    copy(part_all.at[rest], part_all.at[rest], o_send, o_recv.at[0], mate_ids[0]).wait_send()


def shards(queries, key_cache, value_cache, tile_page, row_last):
    groups = lax.axis_size("blk") // KV_HEADS
    blocks = lax.axis_size("blk")
    rows, width = queries.shape
    tokens = key_cache.shape[0]
    block = width // HEAD_DIM // KV_HEADS * rows
    bf16, f32 = jnp.bfloat16, jnp.float32
    dma = pltpu.SemaphoreType.DMA
    quad, one = dma((KV_HEADS,)), dma
    return pl.pallas_call(
        functools.partial(kernel, groups),
        out_shape=jax.ShapeDtypeStruct((rows, width), bf16),
        in_specs=[pl.BlockSpec(memory_space=pltpu.HBM)] * 5,
        out_specs=pl.BlockSpec(memory_space=pltpu.VMEM),
        scratch_shapes=[
            pltpu.VMEM((rows, width), bf16),
            pltpu.VMEM(value_cache.shape, bf16),
            pltpu.SMEM((rows,), jnp.int32),
            pltpu.VMEM((KV_HEADS, block, HEAD_DIM), bf16),
            pltpu.VMEM((1, 128), jnp.int32),
            pltpu.VMEM((groups, KV_HEADS, block, HEAD_DIM), bf16),
            pltpu.VMEM((KV_HEADS, tokens, HEAD_DIM), bf16),
            pltpu.VMEM((KV_HEADS, HEAD_DIM, tokens), bf16),
            pltpu.VMEM((KV_HEADS, HEAD_DIM, tokens), bf16),
            pltpu.VMEM((KV_HEADS, 1, tokens), jnp.int32),
            pltpu.VMEM((blocks, 1, 128), jnp.int32),
            pltpu.VMEM((KV_HEADS, tokens, HEAD_DIM), f32),
            pltpu.VMEM((blocks, block, HEAD_DIM), bf16),
            pltpu.VMEM((blocks, block, HEAD_DIM), bf16),
            pltpu.VMEM((blocks, 1, 128), f32),
            pltpu.VMEM((blocks, 1, 128), f32),
            pltpu.VMEM((blocks, block, HEAD_DIM), f32),
            dma((2,)), dma((3,)),
            quad, dma((blocks,)), dma((groups, 4)), quad, quad, quad, quad,
            one, one, one, one, one, dma((groups,)), one, one,
        ],
        compiler_params=pltpu.CompilerParams(
            collective_id=0, has_side_effects=True, vmem_limit_bytes=55104 * 1024
        ),
        cost_estimate=pl.CostEstimate(flops=540_000_000, bytes_accessed=700_000, transcendentals=1_000_000),
    )(queries, key_cache, value_cache, tile_page.reshape(1, tokens), row_last)


def solution(mesh):
    placed = (
        P(("parts", "blk"), None),
        P(("parts", "blk"), None),
        P(("parts", "blk"), None),
        P(("parts", "blk")),
        P(("parts", "blk")),
    )
    return jax.shard_map(
        shards, mesh=mesh, in_specs=placed, out_specs=P(("parts", "blk"), None), check_vma=False
    )
```
